32 devices in a mesh: seg: 8 (over z, y), grp: 4 (over x, core).
Axes of the slice: x: 2, y: 2, z: 4, core: 2. Of those that a mesh axis runs over, the one named last changes fastest.
Arguments:
- tokens: bfloat16 [16384, 1024], P(('seg', 'grp')), may hold values from -72 to 72
- w_qkv: bfloat16 [1024, 3072], replicated, may hold values from -0.1875 to 0.1875
- w_out: bfloat16 [1024, 1024], replicated, may hold values from -0.1875 to 0.1875
- block_table: int32 [256, 13], P('seg'), may hold values from 0 to 255, as said below
Outputs:
- mixed: bfloat16 [16384, 1024], P(('seg', 'grp'))
The draws below stay inside these ranges and needn't reach their ends.
Inputs may be any that keep to these rules, and one draw needn't show every extreme that they name: `block_table`: with segment s of block b = b // 32: column 0 is b; columns 1 to 9 are distinct other blocks of segment s; column 10 + j (j = 0, 1, 2) lies in segment s xor 2**j, and over the 32 query blocks of one segment it names each block of that partner segment once.
All inputs are finite; a program needn't handle non-finite values.
Results may differ from the reference program's by a relative error of at most 0.003.
The reference program's roundings to bfloat16 on the way (of `projected`, `weights` and `attended`) count: a program that leaves them out, or rounds other values in their place, can miss the bound.
Values may be sent and summed in bfloat16 or wider, within the bound.
A program may use at most 128 MiB of HBM per device.

```python
import jax
import jax.numpy as jnp
from jax import lax

D = 1024
H = 32
HD = 32
BLK = 64
KB = 13
TOKENS = 16384
NBS = 32
NB = 256
N_SEG = 8


def draw_tokens(key, part):
    key = jax.random.fold_in(key, 11)
    key_base = jax.random.fold_in(key, 0)
    return jnp.clip(jax.random.normal(key_base, (TOKENS, D), jnp.float32), -6.0, 6.0).astype(jnp.bfloat16)


def draw_block_table(key, part):
    key = jax.random.fold_in(key, 23)
    key_local, key_cross = jax.random.split(key)
    block_ids = jnp.arange(NB, dtype=jnp.int32)
    segment = block_ids // NBS
    own_pos = block_ids % NBS
    columns = jnp.arange(NBS, dtype=jnp.int32)
    scores_int = jax.random.randint(key_local, (NB, NBS), 0, 1 << 20) * NBS + columns[None, :]
    scores_int = jnp.where(columns[None, :] == own_pos[:, None], -1, scores_int)
    chosen = lax.top_k(scores_int, KB - 4)[1].astype(jnp.int32)
    local_cols = segment[:, None] * NBS + chosen
    seg_count = NB // NBS
    order_scores = jax.random.randint(key_cross, (seg_count, 3, NBS), 0, 1 << 20) * NBS + columns
    orders = jnp.argsort(order_scores, axis=-1).astype(jnp.int32)
    partner_cols = []
    for bit_place in range(3):
        partner = jnp.bitwise_xor(segment, 1 << bit_place)
        partner_cols.append(orders[segment, bit_place, own_pos] + partner * NBS)
    return jnp.concatenate([block_ids[:, None], local_cols, jnp.stack(partner_cols, axis=1)], axis=1).astype(jnp.int32)


def noise(stream_key, shape, deviation, most, kind=jnp.bfloat16):
    values = deviation * jax.random.normal(stream_key, shape, jnp.float32)
    return jnp.clip(values, min=-most, max=most).astype(kind)


def setup_inputs(seed: int = 0) -> dict:
    key_list = jax.random.split(jax.random.key(seed), 5)
    tokens = draw_tokens(jax.random.fold_in(key_list[4], 71), 0)
    w_qkv = noise(key_list[1], (D, 3 * D), D ** -0.5, 0.1875)
    w_out = noise(key_list[2], (D, D), D ** -0.5, 0.1875)
    block_table = draw_block_table(jax.random.fold_in(key_list[4], 71), 0)
    return dict(tokens=tokens, w_qkv=w_qkv, w_out=w_out, block_table=block_table)


def attend(query, keys, values, block_table, group_size):
    block_count = query.shape[0]
    head_count = query.shape[2]
    group_count = block_count // group_size
    score_scale = HD ** -0.5
    query_grp = query.reshape(group_count, group_size, BLK, head_count, HD)
    table_grp = block_table.reshape(group_count, group_size, KB)

    def one_group(payload):
        query_blk, table_blk = payload
        key_blk = keys[table_blk].reshape(group_size, KB * BLK, head_count, HD)
        value_blk = values[table_blk].reshape(group_size, KB * BLK, head_count, HD)
        scores = jnp.einsum("gthd,gkhd->ghtk", query_blk.astype(jnp.float32), key_blk.astype(jnp.float32)) * score_scale
        row_max = jnp.max(scores, axis=-1, keepdims=True)
        exp_scores = jnp.exp(scores - row_max)
        row_total = jnp.sum(exp_scores, axis=-1, keepdims=True)
        weights = exp_scores.astype(jnp.bfloat16)
        result = jnp.einsum("ghtk,gkhd->gthd", weights.astype(jnp.float32), value_blk.astype(jnp.float32))
        result = result / jnp.transpose(row_total, (0, 2, 1, 3))
        return result.astype(jnp.bfloat16)

    mapped = lax.map(one_group, (query_grp, table_grp))
    return mapped.reshape(block_count * BLK, head_count * HD)


def reference(tokens, w_qkv, w_out, block_table):
    projected = jnp.dot(tokens, w_qkv, preferred_element_type=jnp.float32).astype(jnp.bfloat16)
    block_count = tokens.shape[0] // BLK
    seg_blocks = block_count // N_SEG
    group_size = min(seg_blocks, max(1, 512 // BLK))
    split_cols = projected.reshape(block_count, BLK, 3, H, HD)
    attended = attend(split_cols[:, :, 0], split_cols[:, :, 1], split_cols[:, :, 2], block_table, group_size)
    return jnp.dot(attended, w_out, preferred_element_type=jnp.float32).astype(jnp.bfloat16)
```

```python
import functools

import jax
import jax.numpy as jnp
from jax import lax
from jax.experimental import pallas as pl
from jax.experimental.pallas import tpu as pltpu
from jax.sharding import PartitionSpec as P

H = 32
HD = 32
BLK = 64
KB = 13
N_PARTNER = 3
N_OWN = KB - N_PARTNER
LANES = 256
LOG2E = 1.4426950408889634


def exchange(value, axis, mask):
    pairs = [(source, source ^ mask) for source in range(lax.axis_size(axis))]
    return lax.ppermute(value, axis, pairs)


def gather_shards(value, axis):
    held = {0: value}
    mask = lax.axis_size(axis) // 2
    while mask >= 1:
        for k in list(held):
            held[k ^ mask] = exchange(held[k], axis, mask)
        mask //= 2
    return [held[k] for k in range(len(held))]


def pick_body(index_ref, rows_ref, out_ref):
    out_ref[...] = rows_ref[...]


def pick_blocks(rows, index):
    count = index.shape[0]
    width = rows.shape[1]
    return pl.pallas_call(
        pick_body,
        grid_spec=pltpu.PrefetchScalarGridSpec(
            num_scalar_prefetch=1,
            grid=(count,),
            in_specs=[pl.BlockSpec((BLK, width), lambda i, index: (index[i], 0))],
            out_specs=pl.BlockSpec((BLK, width), lambda i, index: (i, 0)),
        ),
        out_shape=jax.ShapeDtypeStruct((count * BLK, width), rows.dtype),
        cost_estimate=pl.CostEstimate(
            flops=0, bytes_accessed=4 * count * BLK * width, transcendentals=0
        ),
    )(index, rows)


def attend_body(index_ref, q_ref, ko_ref, vo_ref, *refs):
    kc_refs = refs[:N_PARTNER]
    vc_refs = refs[N_PARTNER : 2 * N_PARTNER]
    out_ref, k_buf, v_buf = refs[2 * N_PARTNER :]
    block = pl.program_id(1)
    for c in range(N_OWN):
        start = pl.multiple_of(index_ref[block * N_OWN + c] * BLK, BLK)
        k_buf[c * BLK : (c + 1) * BLK, :] = ko_ref[pl.ds(start, BLK), :]
        v_buf[c * BLK : (c + 1) * BLK, :] = vo_ref[pl.ds(start, BLK), :]
    for j in range(N_PARTNER):
        c = N_OWN + j
        k_buf[c * BLK : (c + 1) * BLK, :] = kc_refs[j][...]
        v_buf[c * BLK : (c + 1) * BLK, :] = vc_refs[j][...]
    q = q_ref[...]
    head = lax.broadcasted_iota(jnp.int32, (BLK, LANES), 1) // HD
    heads = LANES // HD
    zero = jnp.zeros_like(q)
    spread = jnp.concatenate([jnp.where(head == h, q, zero) for h in range(heads)], axis=0)
    raw = lax.dot_general(
        spread, k_buf[...], (((1,), (1,)), ((), ())), preferred_element_type=jnp.float32
    )
    factor = HD ** (-0.5) * LOG2E
    top = jnp.max(raw, axis=1, keepdims=True) * factor
    exps = jnp.exp2(raw * factor - top)
    total = jnp.sum(exps, axis=1, keepdims=True)
    result = jnp.dot(
        exps.astype(jnp.bfloat16), v_buf[...], preferred_element_type=jnp.float32
    )
    result = result / total
    out = result[0:BLK]
    for h in range(1, heads):
        out = jnp.where(head == h, result[h * BLK : (h + 1) * BLK], out)
    out_ref[...] = out.astype(jnp.bfloat16)


def attend(index, query, own, crosses):
    rows, width = query.shape
    lane_groups = width // LANES
    blocks = rows // BLK
    own_rows = own.shape[0]
    here = lambda hg, i, index: (i, hg)
    value_here = lambda hg, i, index: (i, lane_groups + hg)
    keys = blocks * KB * BLK
    return pl.pallas_call(
        attend_body,
        grid_spec=pltpu.PrefetchScalarGridSpec(
            num_scalar_prefetch=1,
            grid=(lane_groups, blocks),
            in_specs=[
                pl.BlockSpec((BLK, LANES), here),
                pl.BlockSpec((own_rows, LANES), lambda hg, i, index: (0, hg)),
                pl.BlockSpec((own_rows, LANES), lambda hg, i, index: (0, lane_groups + hg)),
            ]
            + [pl.BlockSpec((BLK, LANES), here)] * N_PARTNER
            + [pl.BlockSpec((BLK, LANES), value_here)] * N_PARTNER,
            out_specs=pl.BlockSpec((BLK, LANES), here),
            scratch_shapes=[pltpu.VMEM((KB * BLK, LANES), jnp.bfloat16)] * 2,
        ),
        out_shape=jax.ShapeDtypeStruct((rows, width), jnp.bfloat16),
        compiler_params=pltpu.CompilerParams(vmem_limit_bytes=48 * 1024 * 1024),
        cost_estimate=pl.CostEstimate(
            flops=4 * BLK * keys * width,
            bytes_accessed=own.size * 2,
            transcendentals=BLK * keys * H,
        ),
    )(index, query, own, own, *crosses, *crosses)


def project(rows, weights):
    return jnp.dot(rows, weights, preferred_element_type=jnp.float32).astype(jnp.bfloat16)


def per_device(tokens, w_qkv, w_out, block_table):
    groups = lax.axis_size("grp")
    me = lax.axis_index("grp")
    tok_rows, width = tokens.shape
    blocks = tok_rows // BLK
    seg_blocks = blocks * groups

    table = lax.dynamic_slice_in_dim(block_table, me * blocks, blocks, axis=0) % seg_blocks
    place = ((table // blocks) ^ me) * blocks + table % blocks
    asked = [exchange(table[:, N_OWN + j], "seg", 1 << j) for j in range(N_PARTNER)]

    shards = gather_shards(tokens, "grp")
    rows = jnp.concatenate(shards, axis=0)
    arrived = []
    for j in reversed(range(N_PARTNER)):
        want = ((asked[j] // blocks) ^ me) * blocks + asked[j] % blocks
        arrived.append(exchange(pick_blocks(rows, want), "seg", 1 << j))
    arrived = arrived[::-1]

    query = project(tokens, w_qkv[:, :width])
    own = project(rows, w_qkv[:, width:])
    crosses = [project(part, w_qkv[:, width:]) for part in arrived]
    attended = attend(place[:, :N_OWN].reshape(-1), query, own, crosses)
    return project(attended, w_out)


def solution(mesh):
    return jax.shard_map(
        per_device,
        mesh=mesh,
        in_specs=(P(("seg", "grp"), None), P(), P(), P("seg", None)),
        out_specs=P(("seg", "grp"), None),
        check_vma=False,
    )
```

```python
import functools

import jax
import jax.numpy as jnp
from jax import lax
from jax.experimental import pallas as pl
from jax.experimental.pallas import tpu as pltpu
from jax.sharding import PartitionSpec as P

H = 32
HD = 32
BLK = 64
KB = 13
N_PARTNER = 3
N_OWN = KB - N_PARTNER
LANES = 256
UNROLL = 2
LOG2E = 1.4426950408889634


def exchange(value, axis, mask):
    pairs = [(source, source ^ mask) for source in range(lax.axis_size(axis))]
    return lax.ppermute(value, axis, pairs)


def gather_shards(value, axis):
    held = {0: value}
    mask = lax.axis_size(axis) // 2
    while mask >= 1:
        for k in list(held):
            held[k ^ mask] = exchange(held[k], axis, mask)
        mask //= 2
    return [held[k] for k in range(len(held))]


def pick_body(index_ref, *refs):
    shard_refs = refs[:-2]
    out_ref, sems = refs[-2:]
    count = out_ref.shape[0] // BLK
    shard_blocks = shard_refs[0].shape[0] // BLK

    def copy_of(i, shard, block):
        return pltpu.make_async_copy(
            shard_refs[shard].at[pl.ds(block * BLK, BLK), :],
            out_ref.at[pl.ds(i * BLK, BLK), :],
            sems.at[i],
        )

    for i in range(count):
        place = index_ref[i]
        for shard in range(len(shard_refs)):

            @pl.when(place // shard_blocks == shard)
            def _():
                copy_of(i, shard, place % shard_blocks).start()

    for i in range(count):
        copy_of(i, 0, 0).wait()


def pick_blocks(shards, index):
    count = index.shape[0]
    width = shards[0].shape[1]
    anywhere = pl.BlockSpec(memory_space=pl.ANY)
    return pl.pallas_call(
        pick_body,
        grid_spec=pltpu.PrefetchScalarGridSpec(
            num_scalar_prefetch=1,
            grid=(1,),
            in_specs=[anywhere] * len(shards),
            out_specs=anywhere,
            scratch_shapes=[pltpu.SemaphoreType.DMA((count,))],
        ),
        out_shape=jax.ShapeDtypeStruct((count * BLK, width), shards[0].dtype),
        cost_estimate=pl.CostEstimate(
            flops=0, bytes_accessed=4 * count * BLK * width, transcendentals=0
        ),
    )(index, *shards)


GROUP_HEADS = LANES // HD
STAT = 128
FACTOR = HD ** (-0.5) * LOG2E


def raw_scores(q, keys):
    head = lax.broadcasted_iota(jnp.int32, (BLK, LANES), 1) // HD
    zero = jnp.zeros_like(q)
    spread = jnp.concatenate(
        [jnp.where(head == h, q, zero) for h in range(GROUP_HEADS)], axis=0
    )
    return lax.dot_general(
        spread, keys, (((1,), (1,)), ((), ())), preferred_element_type=jnp.float32
    )


def fold(values, lane_head):
    shape = lane_head.shape
    out = jnp.broadcast_to(values[0:BLK], shape)
    for h in range(1, GROUP_HEADS):
        out = jnp.where(lane_head == h, values[h * BLK : (h + 1) * BLK], out)
    return out


def own_body(unroll, shard_count, index_ref, q_ref, *refs):
    shard_refs = refs[: 2 * shard_count]
    part_ref, stat_ref, k_all, v_all, k_buf, v_buf = refs[2 * shard_count :]
    step = pl.program_id(1)
    shard_rows = shard_refs[0].shape[0]

    @pl.when(step == 0)
    def _():
        for s in range(shard_count):
            here = slice(s * shard_rows, (s + 1) * shard_rows)
            k_all[here, :] = shard_refs[s][...]
            v_all[here, :] = shard_refs[shard_count + s][...]

    head = lax.broadcasted_iota(jnp.int32, (BLK, LANES), 1) // HD
    stat_lane = lax.broadcasted_iota(jnp.int32, (BLK, STAT), 1)
    for u in range(unroll):
        block = step * unroll + u
        for c in range(N_OWN):
            start = pl.multiple_of(index_ref[block * N_OWN + c] * BLK, BLK)
            k_buf[u, c * BLK : (c + 1) * BLK, :] = k_all[pl.ds(start, BLK), :]
            v_buf[u, c * BLK : (c + 1) * BLK, :] = v_all[pl.ds(start, BLK), :]
        rows = slice(u * BLK, (u + 1) * BLK)
        raw = raw_scores(q_ref[rows, :], k_buf[u])
        top = jnp.max(raw, axis=1, keepdims=True) * FACTOR
        exps = jnp.exp2(raw * FACTOR - top)
        total = jnp.sum(exps, axis=1, keepdims=True)
        result = jnp.dot(
            exps.astype(jnp.bfloat16), v_buf[u], preferred_element_type=jnp.float32
        )
        part_ref[rows, :] = fold(result, head)
        stat_ref[rows, :] = jnp.where(
            stat_lane < GROUP_HEADS,
            fold(top, stat_lane),
            fold(total, stat_lane - GROUP_HEADS),
        )


def attend_own(index, query, own, unroll):
    rows, width = query.shape
    lane_groups = width // LANES
    blocks = rows // BLK
    shard_rows = own[0].shape[0]
    own_rows = shard_rows * len(own)
    here = lambda hg, i, index: (i, hg)
    keys = N_OWN * BLK
    return pl.pallas_call(
        functools.partial(own_body, unroll, len(own)),
        grid_spec=pltpu.PrefetchScalarGridSpec(
            num_scalar_prefetch=1,
            grid=(lane_groups, blocks // unroll),
            in_specs=[pl.BlockSpec((unroll * BLK, LANES), here)]
            + [pl.BlockSpec((shard_rows, LANES), lambda hg, i, index: (0, hg))] * len(own)
            + [pl.BlockSpec((shard_rows, LANES), lambda hg, i, index: (0, lane_groups + hg))]
            * len(own),
            out_specs=[
                pl.BlockSpec((unroll * BLK, LANES), here),
                pl.BlockSpec((unroll * BLK, STAT), here),
            ],
            scratch_shapes=[pltpu.VMEM((own_rows, LANES), jnp.bfloat16)] * 2
            + [pltpu.VMEM((unroll, keys, LANES), jnp.bfloat16)] * 2,
        ),
        out_shape=[
            jax.ShapeDtypeStruct((rows, width), jnp.float32),
            jax.ShapeDtypeStruct((rows, lane_groups * STAT), jnp.float32),
        ],
        compiler_params=pltpu.CompilerParams(vmem_limit_bytes=48 * 1024 * 1024),
        cost_estimate=pl.CostEstimate(
            flops=4 * rows * keys * width * GROUP_HEADS,
            bytes_accessed=own_rows * width * 4,
            transcendentals=rows * keys * H,
        ),
    )(index, query, *own, *own)


def cross_body(unroll, q_ref, part_ref, stat_ref, *refs):
    k_refs = refs[:N_PARTNER]
    v_refs = refs[N_PARTNER : 2 * N_PARTNER]
    out_ref = refs[2 * N_PARTNER]
    head = lax.broadcasted_iota(jnp.int32, (BLK, LANES), 1) // HD
    for u in range(unroll):
        rows = slice(u * BLK, (u + 1) * BLK)
        keys = jnp.concatenate([ref[rows, :] for ref in k_refs], axis=0)
        values = jnp.concatenate([ref[rows, :] for ref in v_refs], axis=0)
        raw = raw_scores(q_ref[rows, :], keys)
        stat = stat_ref[rows, :]
        own_top = jnp.concatenate(
            [stat[:, h : h + 1] for h in range(GROUP_HEADS)], axis=0
        )
        own_total = jnp.concatenate(
            [stat[:, GROUP_HEADS + h : GROUP_HEADS + h + 1] for h in range(GROUP_HEADS)],
            axis=0,
        )
        top = jnp.maximum(jnp.max(raw, axis=1, keepdims=True) * FACTOR, own_top)
        exps = jnp.exp2(raw * FACTOR - top)
        scale = jnp.exp2(own_top - top)
        total = jnp.sum(exps, axis=1, keepdims=True) + own_total * scale
        result = jnp.dot(
            exps.astype(jnp.bfloat16), values, preferred_element_type=jnp.float32
        )
        joint = fold(result, head) + part_ref[rows, :] * fold(scale, head)
        out_ref[rows, :] = (joint / fold(total, head)).astype(jnp.bfloat16)


def attend_cross(query, part, stat, crosses, unroll):
    rows, width = query.shape
    lane_groups = width // LANES
    blocks = rows // BLK
    here = lambda hg, i: (i, hg)
    keys = N_PARTNER * BLK
    wide = pl.BlockSpec((unroll * BLK, LANES), here)
    return pl.pallas_call(
        functools.partial(cross_body, unroll),
        grid=(lane_groups, blocks // unroll),
        in_specs=[wide, wide, pl.BlockSpec((unroll * BLK, STAT), here)]
        + [wide] * N_PARTNER
        + [pl.BlockSpec((unroll * BLK, LANES), lambda hg, i: (i, lane_groups + hg))]
        * N_PARTNER,
        out_specs=wide,
        out_shape=jax.ShapeDtypeStruct((rows, width), jnp.bfloat16),
        compiler_params=pltpu.CompilerParams(vmem_limit_bytes=48 * 1024 * 1024),
        cost_estimate=pl.CostEstimate(
            flops=4 * rows * keys * width * GROUP_HEADS,
            bytes_accessed=rows * width * 20,
            transcendentals=rows * keys * H,
        ),
    )(query, part, stat, *crosses, *crosses)


def project(rows, weights):
    return jnp.dot(rows, weights, preferred_element_type=jnp.float32).astype(jnp.bfloat16)


def per_device(tokens, w_qkv, w_out, block_table):
    groups = lax.axis_size("grp")
    me = lax.axis_index("grp")
    tok_rows, width = tokens.shape
    blocks = tok_rows // BLK
    seg_blocks = blocks * groups

    table = lax.dynamic_slice_in_dim(block_table, me * blocks, blocks, axis=0) % seg_blocks
    place = ((table // blocks) ^ me) * blocks + table % blocks
    asked = [exchange(table[:, N_OWN + j], "seg", 1 << j) for j in range(N_PARTNER)]

    shards = gather_shards(tokens, "grp")
    arrived = []
    for j in reversed(range(N_PARTNER)):
        want = ((asked[j] // blocks) ^ me) * blocks + asked[j] % blocks
        arrived.append(exchange(pick_blocks(shards, want), "seg", 1 << j))
    arrived = arrived[::-1]

    query = project(tokens, w_qkv[:, :width])
    own = [project(shard, w_qkv[:, width:]) for shard in shards]
    part, stat = attend_own(place[:, :N_OWN].reshape(-1), query, own, UNROLL)
    crosses = [project(rows, w_qkv[:, width:]) for rows in arrived]
    attended = attend_cross(query, part, stat, crosses, UNROLL)
    return project(attended, w_out)


def solution(mesh):
    return jax.shard_map(
        per_device,
        mesh=mesh,
        in_specs=(P(("seg", "grp"), None), P(), P(), P("seg", None)),
        out_specs=P(("seg", "grp"), None),
        check_vma=False,
    )
```

```python
import functools

import jax
import jax.numpy as jnp
from jax import lax
from jax.experimental import pallas as pl
from jax.experimental.pallas import tpu as pltpu
from jax.sharding import PartitionSpec as P

H = 32
HD = 32
BLK = 64
KB = 13
N_PARTNER = 3
N_OWN = KB - N_PARTNER
LANES = 256
UNROLL = 2
PARTS = 2
LOG2E = 1.4426950408889634


def exchange(value, axis, mask):
    pairs = [(source, source ^ mask) for source in range(lax.axis_size(axis))]
    return lax.ppermute(value, axis, pairs)


def gather_shards(value, axis):
    held = {0: value}
    mask = lax.axis_size(axis) // 2
    while mask >= 1:
        for k in list(held):
            held[k ^ mask] = exchange(held[k], axis, mask)
        mask //= 2
    return [held[k] for k in range(len(held))]


def pick_body(index_ref, *refs):
    shard_refs = refs[: -N_PARTNER - 1]
    out_refs = refs[-N_PARTNER - 1 : -1]
    sems = refs[-1]
    count = out_refs[0].shape[0] // BLK
    shard_blocks = shard_refs[0].shape[0] // BLK

    def copy_of(j, i, shard, block):
        return pltpu.make_async_copy(
            shard_refs[shard].at[pl.ds(pl.multiple_of(block * BLK, BLK), BLK), :],
            out_refs[j].at[pl.ds(i * BLK, BLK), :],
            sems.at[j * count + i],
        )

    for j in range(N_PARTNER):
        for i in range(count):
            place = index_ref[j * count + i]
            for shard in range(len(shard_refs)):

                @pl.when(place // shard_blocks == shard)
                def _():
                    copy_of(j, i, shard, place % shard_blocks).start()

    for j in range(N_PARTNER):
        for i in range(count):
            copy_of(j, i, 0, 0).wait()


def pick_blocks(shards, index):
    count = index.shape[0] // N_PARTNER
    width = shards[0].shape[1]
    return pl.pallas_call(
        pick_body,
        grid_spec=pltpu.PrefetchScalarGridSpec(
            num_scalar_prefetch=1,
            grid=(1,),
            in_specs=[pl.BlockSpec(memory_space=pl.ANY)] * len(shards),
            out_specs=[pl.BlockSpec((count * BLK, width), lambda i, index: (0, 0))] * N_PARTNER,
            scratch_shapes=[pltpu.SemaphoreType.DMA((N_PARTNER * count,))],
        ),
        out_shape=[jax.ShapeDtypeStruct((count * BLK, width), shards[0].dtype)] * N_PARTNER,
        compiler_params=pltpu.CompilerParams(vmem_limit_bytes=32 * 1024 * 1024),
        cost_estimate=pl.CostEstimate(
            flops=0, bytes_accessed=4 * N_PARTNER * count * BLK * width, transcendentals=0
        ),
    )(index, *shards)


GROUP_HEADS = LANES // HD
FACTOR = HD ** (-0.5) * LOG2E


def attend_body(unroll, shard_count, index_ref, q_ref, *refs):
    shard_refs = refs[: 2 * shard_count]
    refs = refs[2 * shard_count :]
    kc_refs = refs[:N_PARTNER]
    vc_refs = refs[N_PARTNER : 2 * N_PARTNER]
    out_ref, k_all, v_all, k_buf, v_buf = refs[2 * N_PARTNER :]
    step = pl.program_id(1)
    shard_rows = shard_refs[0].shape[0]

    @pl.when(step == 0)
    def _():
        for s in range(shard_count):
            here = slice(s * shard_rows, (s + 1) * shard_rows)
            k_all[here, :] = shard_refs[s][...]
            v_all[here, :] = shard_refs[shard_count + s][...]

    head = lax.broadcasted_iota(jnp.int32, (BLK, LANES), 1) // HD
    for u in range(unroll):
        rows = slice(u * BLK, (u + 1) * BLK)
        for c in range(KB):
            here = slice(c * BLK, (c + 1) * BLK)
            if c < N_OWN:
                place = index_ref[(step * unroll + u) * N_OWN + c]
                there = pl.ds(pl.multiple_of(place * BLK, BLK), BLK)
                k_buf[u, here, :] = k_all[there, :]
                v_buf[u, here, :] = v_all[there, :]
            else:
                k_buf[u, here, :] = kc_refs[c - N_OWN][rows, :]
                v_buf[u, here, :] = vc_refs[c - N_OWN][rows, :]
    for u in range(unroll):
        rows = slice(u * BLK, (u + 1) * BLK)
        q = q_ref[rows, :]
        zero = jnp.zeros_like(q)
        spread = jnp.concatenate(
            [jnp.where(head == h, q, zero) for h in range(GROUP_HEADS)], axis=0
        )
        raw = lax.dot_general(
            spread, k_buf[u], (((1,), (1,)), ((), ())), preferred_element_type=jnp.float32
        )
        top = jnp.max(raw, axis=1, keepdims=True) * FACTOR
        exps = jnp.exp2(raw * FACTOR - top)
        total = jnp.sum(exps, axis=1, keepdims=True)
        result = jnp.dot(
            exps.astype(jnp.bfloat16), v_buf[u], preferred_element_type=jnp.float32
        )
        result = result / total
        out = result[0:BLK]
        for h in range(1, GROUP_HEADS):
            out = jnp.where(head == h, result[h * BLK : (h + 1) * BLK], out)
        out_ref[rows, :] = out.astype(jnp.bfloat16)


def attend(index, query, first, own, crosses):
    rows = crosses[0].shape[0]
    width = query.shape[1]
    lane_groups = width // LANES
    blocks = rows // BLK
    unroll = min(UNROLL, blocks)
    shard_rows = own[0].shape[0]
    own_rows = shard_rows * len(own)
    here = lambda hg, i, index: (i, hg)
    value_here = lambda hg, i, index: (i, lane_groups + hg)
    skip = first // unroll
    keys = KB * BLK
    part = (unroll * BLK, LANES)
    return pl.pallas_call(
        functools.partial(attend_body, unroll, len(own)),
        grid_spec=pltpu.PrefetchScalarGridSpec(
            num_scalar_prefetch=1,
            grid=(lane_groups, blocks // unroll),
            in_specs=[pl.BlockSpec(part, lambda hg, i, index: (skip + i, hg))]
            + [pl.BlockSpec((shard_rows, LANES), lambda hg, i, index: (0, hg))] * len(own)
            + [pl.BlockSpec((shard_rows, LANES), lambda hg, i, index: (0, lane_groups + hg))]
            * len(own)
            + [pl.BlockSpec(part, here)] * N_PARTNER
            + [pl.BlockSpec(part, value_here)] * N_PARTNER,
            out_specs=pl.BlockSpec(part, here),
            scratch_shapes=[pltpu.VMEM((own_rows, LANES), jnp.bfloat16)] * 2
            + [pltpu.VMEM((unroll, keys, LANES), jnp.bfloat16)] * 2,
        ),
        out_shape=jax.ShapeDtypeStruct((rows, width), jnp.bfloat16),
        compiler_params=pltpu.CompilerParams(vmem_limit_bytes=48 * 1024 * 1024),
        cost_estimate=pl.CostEstimate(
            flops=4 * rows * keys * width * GROUP_HEADS,
            bytes_accessed=own_rows * width * 4,
            transcendentals=rows * keys * H,
        ),
    )(index, query, *own, *own, *crosses, *crosses)


def project(rows, weights):
    return jnp.dot(rows, weights, preferred_element_type=jnp.float32).astype(jnp.bfloat16)


def per_device(tokens, w_qkv, w_out, block_table):
    groups = lax.axis_size("grp")
    me = lax.axis_index("grp")
    tok_rows, width = tokens.shape
    blocks = tok_rows // BLK
    seg_blocks = blocks * groups

    table = lax.dynamic_slice_in_dim(block_table, me * blocks, blocks, axis=0) % seg_blocks
    place = ((table // blocks) ^ me) * blocks + table % blocks
    asked = [exchange(table[:, N_OWN + j], "seg", 1 << j) for j in range(N_PARTNER)]

    shards = gather_shards(tokens, "grp")
    want = [((a // blocks) ^ me) * blocks + a % blocks for a in asked]
    size = blocks // PARTS
    picked = []
    for part in range(PARTS):
        here = slice(part * size, (part + 1) * size)
        picked.append(pick_blocks(shards, jnp.concatenate([w[here] for w in want])))
    arrived = [
        [exchange(rows, "seg", 1 << j) for j, rows in enumerate(parts)] for parts in picked
    ]

    w_q, w_kv = w_qkv[:, :width], w_qkv[:, width:]
    query = project(tokens, w_q)
    own = [project(shard, w_kv) for shard in shards]
    mixed = []
    for part in range(PARTS):
        first = part * size
        index = place[first : first + size, :N_OWN].reshape(-1)
        crosses = [project(rows, w_kv) for rows in arrived[part]]
        mixed.append(project(attend(index, query, first, own, crosses), w_out))
    return jnp.concatenate(mixed, axis=0)


def solution(mesh):
    return jax.shard_map(
        per_device,
        mesh=mesh,
        in_specs=(P(("seg", "grp"), None), P(), P(), P("seg", None)),
        out_specs=P(("seg", "grp"), None),
        check_vma=False,
    )
```

```python
import functools

import jax
import jax.numpy as jnp
from jax import lax
from jax.experimental import pallas as pl
from jax.experimental.pallas import tpu as pltpu
from jax.sharding import PartitionSpec as P

H = 32
HD = 32
BLK = 64
KB = 13
N_PARTNER = 3
N_OWN = KB - N_PARTNER
LANES = 256
UNROLL = 2
PARTS = 2
LOG2E = 1.4426950408889634


def exchange(value, axis, mask):
    pairs = [(source, source ^ mask) for source in range(lax.axis_size(axis))]
    return lax.ppermute(value, axis, pairs)


def gather_shards(value, axis):
    held = {0: value}
    mask = lax.axis_size(axis) // 2
    while mask >= 1:
        for k in list(held):
            held[k ^ mask] = exchange(held[k], axis, mask)
        mask //= 2
    return [held[k] for k in range(len(held))]


def pick_body(index_ref, *refs):
    shard_refs = refs[: -N_PARTNER - 1]
    out_refs = refs[-N_PARTNER - 1 : -1]
    sems = refs[-1]
    count = out_refs[0].shape[0] // BLK
    shard_blocks = shard_refs[0].shape[0] // BLK

    def copy_of(j, i, shard, block):
        return pltpu.make_async_copy(
            shard_refs[shard].at[pl.ds(pl.multiple_of(block * BLK, BLK), BLK), :],
            out_refs[j].at[pl.ds(i * BLK, BLK), :],
            sems.at[j * count + i],
        )

    for j in range(N_PARTNER):
        for i in range(count):
            place = index_ref[j * count + i]
            for shard in range(len(shard_refs)):

                @pl.when(place // shard_blocks == shard)
                def _():
                    copy_of(j, i, shard, place % shard_blocks).start()

    for j in range(N_PARTNER):
        for i in range(count):
            copy_of(j, i, 0, 0).wait()


def pick_blocks(shards, index):
    count = index.shape[0] // N_PARTNER
    width = shards[0].shape[1]
    return pl.pallas_call(
        pick_body,
        grid_spec=pltpu.PrefetchScalarGridSpec(
            num_scalar_prefetch=1,
            grid=(1,),
            in_specs=[pl.BlockSpec(memory_space=pl.ANY)] * len(shards),
            out_specs=[pl.BlockSpec((count * BLK, width), lambda i, index: (0, 0))] * N_PARTNER,
            scratch_shapes=[pltpu.SemaphoreType.DMA((N_PARTNER * count,))],
        ),
        out_shape=[jax.ShapeDtypeStruct((count * BLK, width), shards[0].dtype)] * N_PARTNER,
        compiler_params=pltpu.CompilerParams(vmem_limit_bytes=32 * 1024 * 1024),
        cost_estimate=pl.CostEstimate(
            flops=0, bytes_accessed=4 * N_PARTNER * count * BLK * width, transcendentals=0
        ),
    )(index, *shards)


GROUP_HEADS = LANES // HD
FACTOR = HD ** (-0.5) * LOG2E


def attend_body(unroll, shard_count, index_ref, q_ref, *refs):
    shard_refs = refs[: 2 * shard_count]
    refs = refs[2 * shard_count :]
    kc_refs = refs[:N_PARTNER]
    vc_refs = refs[N_PARTNER : 2 * N_PARTNER]
    out_ref, k_all, v_all, k_buf, v_buf = refs[2 * N_PARTNER :]
    step = pl.program_id(1)
    shard_rows = shard_refs[0].shape[0]

    @pl.when(step == 0)
    def _():
        for s in range(shard_count):
            here = slice(s * shard_rows, (s + 1) * shard_rows)
            k_all[here, :] = shard_refs[s][...]
            v_all[here, :] = shard_refs[shard_count + s][...]

    head = lax.broadcasted_iota(jnp.int32, (BLK, LANES), 1) // HD
    for u in range(unroll):
        rows = slice(u * BLK, (u + 1) * BLK)
        for c in range(KB):
            here = slice(c * BLK, (c + 1) * BLK)
            if c < N_OWN:
                place = index_ref[(step * unroll + u) * N_OWN + c]
                there = pl.ds(pl.multiple_of(place * BLK, BLK), BLK)
                k_buf[u, here, :] = k_all[there, :]
                v_buf[u, here, :] = v_all[there, :]
            else:
                k_buf[u, here, :] = kc_refs[c - N_OWN][rows, :]
                v_buf[u, here, :] = vc_refs[c - N_OWN][rows, :]
    for u in range(unroll):
        rows = slice(u * BLK, (u + 1) * BLK)
        q = q_ref[rows, :]
        zero = jnp.zeros_like(q)
        spread = jnp.concatenate(
            [jnp.where(head == h, q, zero) for h in range(GROUP_HEADS)], axis=0
        )
        raw = lax.dot_general(
            spread, k_buf[u], (((1,), (1,)), ((), ())), preferred_element_type=jnp.float32
        )
        top = jnp.max(raw, axis=1, keepdims=True) * FACTOR
        exps = jnp.exp2(raw * FACTOR - top)
        total = jnp.sum(exps, axis=1, keepdims=True)
        result = jnp.dot(
            exps.astype(jnp.bfloat16), v_buf[u], preferred_element_type=jnp.float32
        )
        result = result / total
        out = result[0:BLK]
        for h in range(1, GROUP_HEADS):
            out = jnp.where(head == h, result[h * BLK : (h + 1) * BLK], out)
        out_ref[rows, :] = out.astype(jnp.bfloat16)


def attend(index, query, first, own, crosses):
    rows = crosses[0].shape[0]
    width = query.shape[1]
    lane_groups = width // LANES
    blocks = rows // BLK
    unroll = min(UNROLL, blocks)
    shard_rows = own[0].shape[0]
    own_rows = shard_rows * len(own)
    here = lambda hg, i, index: (i, hg)
    value_here = lambda hg, i, index: (i, lane_groups + hg)
    skip = first // unroll
    keys = KB * BLK
    part = (unroll * BLK, LANES)
    return pl.pallas_call(
        functools.partial(attend_body, unroll, len(own)),
        grid_spec=pltpu.PrefetchScalarGridSpec(
            num_scalar_prefetch=1,
            grid=(lane_groups, blocks // unroll),
            in_specs=[pl.BlockSpec(part, lambda hg, i, index: (skip + i, hg))]
            + [pl.BlockSpec((shard_rows, LANES), lambda hg, i, index: (0, hg))] * len(own)
            + [pl.BlockSpec((shard_rows, LANES), lambda hg, i, index: (0, lane_groups + hg))]
            * len(own)
            + [pl.BlockSpec(part, here)] * N_PARTNER
            + [pl.BlockSpec(part, value_here)] * N_PARTNER,
            out_specs=pl.BlockSpec(part, here),
            scratch_shapes=[pltpu.VMEM((own_rows, LANES), jnp.bfloat16)] * 2
            + [pltpu.VMEM((unroll, keys, LANES), jnp.bfloat16)] * 2,
        ),
        out_shape=jax.ShapeDtypeStruct((rows, width), jnp.bfloat16),
        compiler_params=pltpu.CompilerParams(vmem_limit_bytes=48 * 1024 * 1024),
        cost_estimate=pl.CostEstimate(
            flops=4 * rows * keys * width * GROUP_HEADS,
            bytes_accessed=own_rows * width * 4,
            transcendentals=rows * keys * H,
        ),
    )(index, query, *own, *own, *crosses, *crosses)


def project(rows, weights):
    return jnp.dot(rows, weights, preferred_element_type=jnp.float32).astype(jnp.bfloat16)


def per_device(tokens, w_qkv, w_out, block_table):
    groups = lax.axis_size("grp")
    me = lax.axis_index("grp")
    tok_rows, width = tokens.shape
    blocks = tok_rows // BLK
    seg_blocks = blocks * groups

    table = lax.dynamic_slice_in_dim(block_table, me * blocks, blocks, axis=0) % seg_blocks
    place = ((table // blocks) ^ me) * blocks + table % blocks
    asked = [exchange(table[:, N_OWN + j], "seg", 1 << j) for j in range(N_PARTNER)]

    shards = gather_shards(tokens, "grp")
    want = [((a // blocks) ^ me) * blocks + a % blocks for a in asked]
    size = blocks // PARTS
    w_q, w_kv = w_qkv[:, :width], w_qkv[:, width:]
    query = project(tokens, w_q)
    own = [project(tokens, w_kv)]
    arrived = []
    for part in range(PARTS):
        here = slice(part * size, (part + 1) * size)
        index = jnp.concatenate([w[here] for w in want])
        if part == 1:
            index, arrived[0] = lax.optimization_barrier((index, arrived[0]))
        picked = pick_blocks(shards, index)
        if part == 0:
            picked, later = lax.optimization_barrier((picked, shards[1:]))
        arrived.append([exchange(rows, "seg", 1 << j) for j, rows in enumerate(picked)])
        if part == 0:
            own += [project(shard, w_kv) for shard in later]
    mixed = []
    for part in range(PARTS):
        first = part * size
        index = place[first : first + size, :N_OWN].reshape(-1)
        crosses = [project(rows, w_kv) for rows in arrived[part]]
        mixed.append(project(attend(index, query, first, own, crosses), w_out))
    return jnp.concatenate(mixed, axis=0)


def solution(mesh):
    return jax.shard_map(
        per_device,
        mesh=mesh,
        in_specs=(P(("seg", "grp"), None), P(), P(), P("seg", None)),
        out_specs=P(("seg", "grp"), None),
        check_vma=False,
    )
```

```python
import functools

import jax
import jax.numpy as jnp
from jax import lax
from jax.experimental import pallas as pl
from jax.experimental.pallas import tpu as pltpu
from jax.sharding import PartitionSpec as P

H = 32
HD = 32
BLK = 64
KB = 13
N_PARTNER = 3
N_OWN = KB - N_PARTNER
LANES = 256
UNROLL = 2
PARTS = 2
LOG2E = 1.4426950408889634


def exchange(value, axis, mask):
    pairs = [(source, source ^ mask) for source in range(lax.axis_size(axis))]
    return lax.ppermute(value, axis, pairs)


def gather_shards(value, axis):
    held = {0: value}
    mask = lax.axis_size(axis) // 2
    while mask >= 1:
        for k in list(held):
            held[k ^ mask] = exchange(held[k], axis, mask)
        mask //= 2
    return [held[k] for k in range(len(held))]


def pick_body(index_ref, *refs):
    shard_refs = refs[: -N_PARTNER - 1]
    out_refs = refs[-N_PARTNER - 1 : -1]
    sems = refs[-1]
    count = out_refs[0].shape[0] // BLK
    shard_blocks = shard_refs[0].shape[0] // BLK

    def copy_of(j, i, shard, block):
        return pltpu.make_async_copy(
            shard_refs[shard].at[pl.ds(pl.multiple_of(block * BLK, BLK), BLK), :],
            out_refs[j].at[pl.ds(i * BLK, BLK), :],
            sems.at[j * count + i],
        )

    for j in range(N_PARTNER):
        for i in range(count):
            place = index_ref[j * count + i]
            for shard in range(len(shard_refs)):

                @pl.when(place // shard_blocks == shard)
                def _():
                    copy_of(j, i, shard, place % shard_blocks).start()

    for j in range(N_PARTNER):
        for i in range(count):
            copy_of(j, i, 0, 0).wait()


def pick_blocks(shards, index):
    count = index.shape[0] // N_PARTNER
    width = shards[0].shape[1]
    return pl.pallas_call(
        pick_body,
        grid_spec=pltpu.PrefetchScalarGridSpec(
            num_scalar_prefetch=1,
            grid=(1,),
            in_specs=[pl.BlockSpec(memory_space=pl.ANY)] * len(shards),
            out_specs=[pl.BlockSpec((count * BLK, width), lambda i, index: (0, 0))] * N_PARTNER,
            scratch_shapes=[pltpu.SemaphoreType.DMA((N_PARTNER * count,))],
        ),
        out_shape=[jax.ShapeDtypeStruct((count * BLK, width), shards[0].dtype)] * N_PARTNER,
        compiler_params=pltpu.CompilerParams(vmem_limit_bytes=32 * 1024 * 1024),
        cost_estimate=pl.CostEstimate(
            flops=0, bytes_accessed=4 * N_PARTNER * count * BLK * width, transcendentals=0
        ),
    )(index, *shards)


GROUP_HEADS = LANES // HD
FACTOR = HD ** (-0.5) * LOG2E


def attend_body(unroll, shard_count, index_ref, q_ref, *refs):
    shard_refs = refs[: 2 * shard_count]
    refs = refs[2 * shard_count :]
    kc_refs = refs[:N_PARTNER]
    vc_refs = refs[N_PARTNER : 2 * N_PARTNER]
    out_ref, k_all, v_all, k_buf, v_buf = refs[2 * N_PARTNER :]
    step = pl.program_id(1)
    shard_rows = shard_refs[0].shape[0]

    @pl.when(step == 0)
    def _():
        for s in range(shard_count):
            here = slice(s * shard_rows, (s + 1) * shard_rows)
            k_all[here, :] = shard_refs[s][...]
            v_all[here, :] = shard_refs[shard_count + s][...]

    head = lax.broadcasted_iota(jnp.int32, (BLK, LANES), 1) // HD
    for u in range(unroll):
        rows = slice(u * BLK, (u + 1) * BLK)
        for c in range(KB):
            here = slice(c * BLK, (c + 1) * BLK)
            if c < N_OWN:
                place = index_ref[(step * unroll + u) * N_OWN + c]
                there = pl.ds(pl.multiple_of(place * BLK, BLK), BLK)
                k_buf[u, here, :] = k_all[there, :]
                v_buf[u, here, :] = v_all[there, :]
            else:
                k_buf[u, here, :] = kc_refs[c - N_OWN][rows, :]
                v_buf[u, here, :] = vc_refs[c - N_OWN][rows, :]
    for u in range(unroll):
        rows = slice(u * BLK, (u + 1) * BLK)
        q = q_ref[rows, :]
        zero = jnp.zeros_like(q)
        spread = jnp.concatenate(
            [jnp.where(head == h, q, zero) for h in range(GROUP_HEADS)], axis=0
        )
        raw = lax.dot_general(
            spread, k_buf[u], (((1,), (1,)), ((), ())), preferred_element_type=jnp.float32
        )
        top = jnp.max(raw, axis=1, keepdims=True) * FACTOR
        exps = jnp.exp2(raw * FACTOR - top)
        total = jnp.sum(exps, axis=1, keepdims=True)
        result = jnp.dot(
            exps.astype(jnp.bfloat16), v_buf[u], preferred_element_type=jnp.float32
        )
        result = result / total
        out = result[0:BLK]
        for h in range(1, GROUP_HEADS):
            out = jnp.where(head == h, result[h * BLK : (h + 1) * BLK], out)
        out_ref[rows, :] = out.astype(jnp.bfloat16)


def attend(index, query, first, own, crosses):
    rows = crosses[0].shape[0]
    width = query.shape[1]
    lane_groups = width // LANES
    blocks = rows // BLK
    unroll = min(UNROLL, blocks)
    shard_rows = own[0].shape[0]
    own_rows = shard_rows * len(own)
    here = lambda hg, i, index: (i, hg)
    value_here = lambda hg, i, index: (i, lane_groups + hg)
    skip = first // unroll
    keys = KB * BLK
    part = (unroll * BLK, LANES)
    return pl.pallas_call(
        functools.partial(attend_body, unroll, len(own)),
        grid_spec=pltpu.PrefetchScalarGridSpec(
            num_scalar_prefetch=1,
            grid=(lane_groups, blocks // unroll),
            in_specs=[pl.BlockSpec(part, lambda hg, i, index: (skip + i, hg))]
            + [pl.BlockSpec((shard_rows, LANES), lambda hg, i, index: (0, hg))] * len(own)
            + [pl.BlockSpec((shard_rows, LANES), lambda hg, i, index: (0, lane_groups + hg))]
            * len(own)
            + [pl.BlockSpec(part, here)] * N_PARTNER
            + [pl.BlockSpec(part, value_here)] * N_PARTNER,
            out_specs=pl.BlockSpec(part, here),
            scratch_shapes=[pltpu.VMEM((own_rows, LANES), jnp.bfloat16)] * 2
            + [pltpu.VMEM((unroll, keys, LANES), jnp.bfloat16)] * 2,
        ),
        out_shape=jax.ShapeDtypeStruct((rows, width), jnp.bfloat16),
        compiler_params=pltpu.CompilerParams(vmem_limit_bytes=48 * 1024 * 1024),
        cost_estimate=pl.CostEstimate(
            flops=4 * rows * keys * width * GROUP_HEADS,
            bytes_accessed=own_rows * width * 4,
            transcendentals=rows * keys * H,
        ),
    )(index, query, *own, *own, *crosses, *crosses)


def project(rows, weights):
    return jnp.dot(rows, weights, preferred_element_type=jnp.float32).astype(jnp.bfloat16)


def per_device(tokens, w_qkv, w_out, block_table):
    groups = lax.axis_size("grp")
    me = lax.axis_index("grp")
    tok_rows, width = tokens.shape
    blocks = tok_rows // BLK
    seg_blocks = blocks * groups

    table = lax.dynamic_slice_in_dim(block_table, me * blocks, blocks, axis=0) % seg_blocks
    place = ((table // blocks) ^ me) * blocks + table % blocks
    asked = [exchange(table[:, N_OWN + j], "seg", 1 << j) for j in range(N_PARTNER)]

    shards = gather_shards(tokens, "grp")
    want = [((a // blocks) ^ me) * blocks + a % blocks for a in asked]
    size = blocks // PARTS
    w_q, w_kv = w_qkv[:, :width], w_qkv[:, width:]
    query = project(tokens, w_q)
    own = [project(tokens, w_kv)]
    arrived = []
    for part in range(PARTS):
        here = slice(part * size, (part + 1) * size)
        index = jnp.concatenate([w[here] for w in want])
        if part == 1:
            index, arrived[0] = lax.optimization_barrier((index, arrived[0]))
        picked = pick_blocks(shards, index)
        arrived.append([exchange(rows, "seg", 1 << j) for j, rows in enumerate(picked)])
        if part == 0:
            arrived[0][0], later = lax.optimization_barrier((arrived[0][0], shards[1:]))
            own += [project(shard, w_kv) for shard in later]
    mixed = []
    for part in range(PARTS):
        first = part * size
        index = place[first : first + size, :N_OWN].reshape(-1)
        crosses = [project(rows, w_kv) for rows in arrived[part]]
        mixed.append(project(attend(index, query, first, own, crosses), w_out))
    return jnp.concatenate(mixed, axis=0)


def solution(mesh):
    return jax.shard_map(
        per_device,
        mesh=mesh,
        in_specs=(P(("seg", "grp"), None), P(), P(), P("seg", None)),
        out_specs=P(("seg", "grp"), None),
        check_vma=False,
    )
```

```python
import functools

import jax
import jax.numpy as jnp
from jax import lax
from jax.experimental import pallas as pl
from jax.experimental.pallas import tpu as pltpu
from jax.sharding import PartitionSpec as P

H = 32
HD = 32
BLK = 64
KB = 13
N_PARTNER = 3
N_OWN = KB - N_PARTNER
LANES = 256
UNROLL = 4
PARTS = 2
LOG2E = 1.4426950408889634


def exchange(value, axis, mask):
    pairs = [(source, source ^ mask) for source in range(lax.axis_size(axis))]
    return lax.ppermute(value, axis, pairs)


def gather_shards(value, axis):
    held = {0: value}
    mask = lax.axis_size(axis) // 2
    while mask >= 1:
        for k in list(held):
            held[k ^ mask] = exchange(held[k], axis, mask)
        mask //= 2
    return [held[k] for k in range(len(held))]


def pick_body(index_ref, *refs):
    shard_refs = refs[: -N_PARTNER - 1]
    out_refs = refs[-N_PARTNER - 1 : -1]
    sems = refs[-1]
    count = out_refs[0].shape[0] // BLK
    shard_blocks = shard_refs[0].shape[0] // BLK

    def copy_of(j, i, shard, block):
        return pltpu.make_async_copy(
            shard_refs[shard].at[pl.ds(pl.multiple_of(block * BLK, BLK), BLK), :],
            out_refs[j].at[pl.ds(i * BLK, BLK), :],
            sems.at[j * count + i],
        )

    for j in range(N_PARTNER):
        for i in range(count):
            place = index_ref[j * count + i]
            for shard in range(len(shard_refs)):

                @pl.when(place // shard_blocks == shard)
                def _():
                    copy_of(j, i, shard, place % shard_blocks).start()

    for j in range(N_PARTNER):
        for i in range(count):
            copy_of(j, i, 0, 0).wait()


def pick_blocks(shards, index):
    count = index.shape[0] // N_PARTNER
    width = shards[0].shape[1]
    return pl.pallas_call(
        pick_body,
        grid_spec=pltpu.PrefetchScalarGridSpec(
            num_scalar_prefetch=1,
            grid=(1,),
            in_specs=[pl.BlockSpec(memory_space=pl.ANY)] * len(shards),
            out_specs=[pl.BlockSpec((count * BLK, width), lambda i, index: (0, 0))] * N_PARTNER,
            scratch_shapes=[pltpu.SemaphoreType.DMA((N_PARTNER * count,))],
        ),
        out_shape=[jax.ShapeDtypeStruct((count * BLK, width), shards[0].dtype)] * N_PARTNER,
        compiler_params=pltpu.CompilerParams(vmem_limit_bytes=32 * 1024 * 1024),
        cost_estimate=pl.CostEstimate(
            flops=0, bytes_accessed=4 * N_PARTNER * count * BLK * width, transcendentals=0
        ),
    )(index, *shards)


GROUP_HEADS = LANES // HD
FACTOR = HD ** (-0.5) * LOG2E


def attend_body(unroll, shard_count, index_ref, q_ref, *refs):
    shard_refs = refs[: 2 * shard_count]
    refs = refs[2 * shard_count :]
    kc_refs = refs[:N_PARTNER]
    vc_refs = refs[N_PARTNER : 2 * N_PARTNER]
    out_ref, k_all, v_all, k_buf, v_buf = refs[2 * N_PARTNER :]
    step = pl.program_id(1)
    shard_rows = shard_refs[0].shape[0]

    @pl.when(step == 0)
    def _():
        for s in range(shard_count):
            here = slice(s * shard_rows, (s + 1) * shard_rows)
            k_all[here, :] = shard_refs[s][...]
            v_all[here, :] = shard_refs[shard_count + s][...]

    head = lax.broadcasted_iota(jnp.int32, (BLK, LANES), 1) // HD
    for u in range(unroll):
        rows = slice(u * BLK, (u + 1) * BLK)
        for c in range(KB):
            here = slice(c * BLK, (c + 1) * BLK)
            if c < N_OWN:
                place = index_ref[(step * unroll + u) * N_OWN + c]
                there = pl.ds(pl.multiple_of(place * BLK, BLK), BLK)
                k_buf[u, here, :] = k_all[there, :]
                v_buf[u, here, :] = v_all[there, :]
            else:
                k_buf[u, here, :] = kc_refs[c - N_OWN][rows, :]
                v_buf[u, here, :] = vc_refs[c - N_OWN][rows, :]
    for u in range(unroll):
        rows = slice(u * BLK, (u + 1) * BLK)
        q = q_ref[rows, :]
        zero = jnp.zeros_like(q)
        spread = jnp.concatenate(
            [jnp.where(head == h, q, zero) for h in range(GROUP_HEADS)], axis=0
        )
        raw = lax.dot_general(
            spread, k_buf[u], (((1,), (1,)), ((), ())), preferred_element_type=jnp.float32
        )
        top = jnp.max(raw, axis=1, keepdims=True) * FACTOR
        exps = jnp.exp2(raw * FACTOR - top)
        total = jnp.sum(exps, axis=1, keepdims=True)
        result = jnp.dot(
            exps.astype(jnp.bfloat16), v_buf[u], preferred_element_type=jnp.float32
        )
        result = result / total
        out = result[0:BLK]
        for h in range(1, GROUP_HEADS):
            out = jnp.where(head == h, result[h * BLK : (h + 1) * BLK], out)
        out_ref[rows, :] = out.astype(jnp.bfloat16)


def attend(index, query, first, own, crosses):
    rows = crosses[0].shape[0]
    width = query.shape[1]
    lane_groups = width // LANES
    blocks = rows // BLK
    unroll = min(UNROLL, blocks)
    shard_rows = own[0].shape[0]
    own_rows = shard_rows * len(own)
    here = lambda hg, i, index: (i, hg)
    value_here = lambda hg, i, index: (i, lane_groups + hg)
    skip = first // unroll
    keys = KB * BLK
    part = (unroll * BLK, LANES)
    return pl.pallas_call(
        functools.partial(attend_body, unroll, len(own)),
        grid_spec=pltpu.PrefetchScalarGridSpec(
            num_scalar_prefetch=1,
            grid=(lane_groups, blocks // unroll),
            in_specs=[pl.BlockSpec(part, lambda hg, i, index: (skip + i, hg))]
            + [pl.BlockSpec((shard_rows, LANES), lambda hg, i, index: (0, hg))] * len(own)
            + [pl.BlockSpec((shard_rows, LANES), lambda hg, i, index: (0, lane_groups + hg))]
            * len(own)
            + [pl.BlockSpec(part, here)] * N_PARTNER
            + [pl.BlockSpec(part, value_here)] * N_PARTNER,
            out_specs=pl.BlockSpec(part, here),
            scratch_shapes=[pltpu.VMEM((own_rows, LANES), jnp.bfloat16)] * 2
            + [pltpu.VMEM((unroll, keys, LANES), jnp.bfloat16)] * 2,
        ),
        out_shape=jax.ShapeDtypeStruct((rows, width), jnp.bfloat16),
        compiler_params=pltpu.CompilerParams(vmem_limit_bytes=48 * 1024 * 1024),
        cost_estimate=pl.CostEstimate(
            flops=4 * rows * keys * width * GROUP_HEADS,
            bytes_accessed=own_rows * width * 4,
            transcendentals=rows * keys * H,
        ),
    )(index, query, *own, *own, *crosses, *crosses)


def project(rows, weights):
    return jnp.dot(rows, weights, preferred_element_type=jnp.float32).astype(jnp.bfloat16)


def per_device(tokens, w_qkv, w_out, block_table):
    groups = lax.axis_size("grp")
    me = lax.axis_index("grp")
    tok_rows, width = tokens.shape
    blocks = tok_rows // BLK
    seg_blocks = blocks * groups

    table = lax.dynamic_slice_in_dim(block_table, me * blocks, blocks, axis=0) % seg_blocks
    place = ((table // blocks) ^ me) * blocks + table % blocks
    asked = [exchange(table[:, N_OWN + j], "seg", 1 << j) for j in range(N_PARTNER)]

    shards = gather_shards(tokens, "grp")
    want = [((a // blocks) ^ me) * blocks + a % blocks for a in asked]
    size = blocks // PARTS
    w_q, w_kv = w_qkv[:, :width], w_qkv[:, width:]
    query = project(tokens, w_q)
    own = [project(tokens, w_kv)]
    arrived = []
    for part in range(PARTS):
        here = slice(part * size, (part + 1) * size)
        index = jnp.concatenate([w[here] for w in want])
        if part == 1:
            index, arrived[0] = lax.optimization_barrier((index, arrived[0]))
        picked = pick_blocks(shards, index)
        arrived.append([exchange(rows, "seg", 1 << j) for j, rows in enumerate(picked)])
        if part == 0:
            arrived[0][0], later = lax.optimization_barrier((arrived[0][0], shards[1:]))
            own += [project(shard, w_kv) for shard in later]
    mixed = []
    for part in range(PARTS):
        first = part * size
        index = place[first : first + size, :N_OWN].reshape(-1)
        crosses = [project(rows, w_kv) for rows in arrived[part]]
        mixed.append(project(attend(index, query, first, own, crosses), w_out))
    return jnp.concatenate(mixed, axis=0)


def solution(mesh):
    return jax.shard_map(
        per_device,
        mesh=mesh,
        in_specs=(P(("seg", "grp"), None), P(), P(), P("seg", None)),
        out_specs=P(("seg", "grp"), None),
        check_vma=False,
    )
```
